32 devices in a mesh: sy: 16 (over z, y, x), sx: 2 (over core).
Axes of the slice: x: 2, y: 2, z: 4, core: 2. Of those that a mesh axis runs over, the one named last changes fastest.
Arguments:
- object_slices: bfloat16 [2, 2, 2048, 2048], P(None, None, 'sy', 'sx'), may hold values from -4 to 4
- probe_wave: float32 [2, 256, 256], replicated, may hold values from -4 to 4
- propagator_phase: float32 [256, 256], replicated, may hold values from -3.140625 to 3.140625
- intensities: bfloat16 [16, 2, 4, 256, 256], P('sy', 'sx'), may hold values from 0 to 2
- scan_offsets: int32 [16, 2, 4, 2], P('sy', 'sx'), may hold values from 0 to 1023, as said below
- live_counts: int32 [16, 2], P('sy', 'sx'), may hold values from 1 to 4, as said below
Outputs:
- object_gradient: float32 [2, 2, 2048, 2048], P(None, None, 'sy', 'sx')
- probe_gradient: float32 [2, 256, 256], replicated
The draws below stay inside these ranges and needn't reach their ends.
Inputs may be any that keep to these rules, and one draw needn't show every extreme that they name: `scan_offsets`: row offsets lie in 0 to 127 and column offsets in 0 to 1023. The first live_counts[u, v] slots of tile (u, v) are live, the rest are not.
All inputs are finite; a program needn't handle non-finite values.
Results may differ from the reference program's by a relative error of at most 0.0004.
Values may be sent and summed in bfloat16 or wider, within the bound.
A program may use at most 128 MiB of HBM per device.

```python
import math
import jax
import jax.numpy as jnp
from jax import lax

W = 256
HALF = 128
SLICES = 2
TY = 128
TX = 1024
P_SIZE = 4
NY = 2048
NX = 2048
N_SY = 16
N_SX = 2


def draw_scan_offsets(key, part):
    key = jax.random.fold_in(key, 11)
    keys = jax.random.split(key, 3)
    rows_drawn = jax.random.randint(keys[0], (N_SY, N_SX, P_SIZE), 0, TY)
    cols_drawn = jax.random.randint(keys[1], (N_SY, N_SX, P_SIZE), 0, TX)
    picks = jax.random.randint(keys[2], (4,), 0, N_SY * N_SX * P_SIZE)
    entry = jnp.arange(N_SY * N_SX * P_SIZE, dtype=jnp.int32).reshape(N_SY, N_SX, P_SIZE)
    rows_drawn = jnp.where(entry == picks[2], 0, rows_drawn)
    rows_drawn = jnp.where(entry == picks[3], TY - 1, rows_drawn)
    cols_drawn = jnp.where(entry == picks[0], 0, cols_drawn)
    cols_drawn = jnp.where(entry == picks[1], TX - 1, cols_drawn)
    return jnp.stack([rows_drawn, cols_drawn], -1).astype(jnp.int32)


def draw_live_counts(key, part):
    key = jax.random.fold_in(key, 23)
    keys = jax.random.split(key, 2)
    levels = jax.random.randint(keys[0], (N_SY, N_SX), 0, 4)
    counts = jnp.maximum(P_SIZE // jnp.left_shift(jnp.int32(1), levels), 1)
    chosen = jax.random.randint(keys[1], (), 0, N_SY * N_SX)
    entry = jnp.arange(N_SY * N_SX, dtype=jnp.int32).reshape(N_SY, N_SX)
    return jnp.where(entry == chosen, P_SIZE, counts).astype(jnp.int32)


def level_of(stream_key, dims, cuts, low, largest):
    def one(dim, parts):
        draws = jax.random.uniform(jax.random.fold_in(jax.random.fold_in(stream_key, 6), dim), (parts,), jnp.float32, low / len(cuts), largest / len(cuts))
        return jnp.repeat(jnp.exp(draws), dims[dim] // parts).reshape((-1,) + (1,) * (len(dims) - dim - 1))

    gain = one(*cuts[0])
    for cut in cuts[1:]:
        gain = gain * one(*cut)
    return gain


def normal_values(rng, dims, scale, reach, shards=(), kind=jnp.bfloat16):
    values = scale * jax.random.normal(rng, dims, jnp.float32)
    if shards:
        values = values * level_of(rng, dims, shards, -0.22, 0.18)
    return jnp.clip(values, -reach, reach).astype(kind)


def setup_inputs(seed: int = 0) -> dict:
    key_of = jax.random.split(jax.random.key(seed), 7)
    object_slices = normal_values(key_of[0], (SLICES, 2, NY, NX), 0.7, 4.0, ((2, 16), (3, 2)))
    probe_wave = normal_values(key_of[1], (2, W, W), 0.7, 4.0, (), jnp.float32)
    propagator_phase = jnp.clip(jax.random.uniform(key_of[2], (W, W), jnp.float32, -3.140625, 3.140625), -3.140625, 3.140625)
    intensities = jnp.clip(2.0 * jax.random.uniform(key_of[3], (N_SY, N_SX, P_SIZE, W, W), jnp.float32) ** level_of(key_of[3], (N_SY, N_SX, P_SIZE, W, W), ((0, 16), (1, 2)), -0.2, 0.2), 0.0, 2.0).astype(jnp.bfloat16)
    scan_offsets = draw_scan_offsets(jax.random.fold_in(key_of[6], 71), 0)
    live_counts = draw_live_counts(jax.random.fold_in(key_of[6], 71), 0)
    return dict(object_slices=object_slices, probe_wave=probe_wave, propagator_phase=propagator_phase, intensities=intensities, scan_offsets=scan_offsets, live_counts=live_counts)


def precise_dot(left, right):
    return jnp.dot(left, right, precision=lax.Precision.HIGHEST, preferred_element_type=jnp.float32)

def dft_tables(window):
    steps = jnp.arange(window, dtype=jnp.int32)
    products = steps[:, None] * steps[None, :] % window
    phases = -2.0 * math.pi / window * products.astype(jnp.float32)
    factor = 1.0 / math.sqrt(window)
    return (jnp.cos(phases) * factor, jnp.sin(phases) * factor)

def transform(value_re, value_im, cos_table, sin_table):
    left_re = precise_dot(cos_table, value_re) - precise_dot(sin_table, value_im)
    left_im = precise_dot(cos_table, value_im) + precise_dot(sin_table, value_re)
    right_re = precise_dot(left_re, cos_table) - precise_dot(left_im, sin_table)
    right_im = precise_dot(left_re, sin_table) + precise_dot(left_im, cos_table)
    return (right_re, right_im)

def one_position(window_block, probe_re, probe_im, prop_re, prop_im, measured, weight, cos_table, sin_table):
    slices = window_block.shape[0]
    wave_re, wave_im = (probe_re, probe_im)
    waves = []
    far_re, far_im = (wave_re, wave_im)
    for s in range(slices):
        waves.append((wave_re, wave_im))
        trans_re, trans_im = (window_block[s, 0], window_block[s, 1])
        exit_re = wave_re * trans_re - wave_im * trans_im
        exit_im = wave_re * trans_im + wave_im * trans_re
        if s < slices - 1:
            spec_re, spec_im = transform(exit_re, exit_im, cos_table, sin_table)
            spec_re, spec_im = (spec_re * prop_re - spec_im * prop_im, spec_re * prop_im + spec_im * prop_re)
            wave_re, wave_im = transform(spec_re, spec_im, cos_table, -sin_table)
        else:
            far_re, far_im = transform(exit_re, exit_im, cos_table, sin_table)
    residual = far_re * far_re + far_im * far_im - measured
    back_re, back_im = transform(2.0 * weight * residual * far_re, 2.0 * weight * residual * far_im, cos_table, -sin_table)
    terms = [None] * slices
    probe_term = None
    for s in reversed(range(slices)):
        wave_re, wave_im = waves[s]
        trans_re, trans_im = (window_block[s, 0], window_block[s, 1])
        terms[s] = jnp.stack([wave_re * back_re + wave_im * back_im, wave_re * back_im - wave_im * back_re])
        carry_re = trans_re * back_re + trans_im * back_im
        carry_im = trans_re * back_im - trans_im * back_re
        if s > 0:
            spec_re, spec_im = transform(carry_re, carry_im, cos_table, sin_table)
            spec_re, spec_im = (spec_re * prop_re + spec_im * prop_im, spec_im * prop_re - spec_re * prop_im)
            back_re, back_im = transform(spec_re, spec_im, cos_table, -sin_table)
        else:
            probe_term = jnp.stack([carry_re, carry_im])
    return (jnp.stack(terms), probe_term)

def reference(object_slices, probe_wave, propagator_phase, intensities, scan_offsets, live_counts):
    cos_table, sin_table = dft_tables(W)
    prop_re = jnp.cos(propagator_phase)
    prop_im = jnp.sin(propagator_phase)
    padded = jnp.pad(object_slices, ((0, 0), (0, 0), (HALF, HALF), (HALF, HALF)))
    entries = N_SY * N_SX * P_SIZE
    flat_offsets = scan_offsets.reshape(entries, 2)
    flat_measured = intensities.reshape(entries, W, W)
    entry = jnp.arange(entries, dtype=jnp.int32)
    tile_row = entry // (N_SX * P_SIZE)
    tile_col = entry // P_SIZE % N_SX
    position = entry % P_SIZE
    counts = live_counts[tile_row, tile_col]
    row_start = (tile_row * TY + flat_offsets[:, 0]).astype(jnp.int32)
    col_start = (tile_col * TX + flat_offsets[:, 1]).astype(jnp.int32)
    weights = jnp.where(position < counts, 1.0, 0.0).astype(jnp.float32)
    zero = jnp.int32(0)

    def visit(carried, record):
        gradient, probe_sum = carried
        row_here, col_here, measured, weight = record
        window_block = lax.dynamic_slice(padded, (zero, zero, row_here, col_here), (SLICES, 2, W, W)).astype(jnp.float32)
        grad_window, grad_probe = one_position(window_block, probe_wave[0], probe_wave[1], prop_re, prop_im, measured.astype(jnp.float32), weight, cos_table, sin_table)
        current = lax.dynamic_slice(gradient, (zero, zero, row_here, col_here), (SLICES, 2, W, W))
        gradient = lax.dynamic_update_slice(gradient, current + grad_window, (zero, zero, row_here, col_here))
        return ((gradient, probe_sum + grad_probe), None)
    start = (jnp.zeros(padded.shape, jnp.float32), jnp.zeros((2, W, W), jnp.float32))
    (gradient, probe_sum), _ = lax.scan(visit, start, (row_start, col_start, flat_measured, weights))
    object_gradient = gradient[:, :, HALF:HALF + NY, HALF:HALF + NX]
    probe_gradient = probe_sum * (1.0 / math.sqrt(P_SIZE * N_SY * N_SX))
    return (object_gradient, probe_gradient)
```

```python
import functools
import math

import jax
import jax.numpy as jnp
import numpy as np
from jax import lax
from jax.experimental import pallas as pl
from jax.experimental.pallas import tpu as pltpu
from jax.sharding import PartitionSpec as P

F32 = jnp.float32
BF16 = jnp.bfloat16
WHOLE = pl.BlockSpec(memory_space=pltpu.VMEM)
SCALARS = pl.BlockSpec(memory_space=pltpu.SMEM)


def passed_along(block, axis, distance):
    devices = range(lax.axis_size(axis))
    route = [(i - distance, i) for i in devices if i - distance in devices]
    return lax.ppermute(block, axis, route)


def split_tables(window):
    half = window // 2
    steps = np.arange(half)
    left, right = [], []

    def parts(matrix):
        high = matrix.astype(np.float32).astype(jnp.bfloat16)
        low = (matrix - high.astype(np.float64)).astype(np.float32).astype(jnp.bfloat16)
        return high, low

    forms = []
    for odd in (0, 1):
        angle = -2.0 * math.pi / window * ((steps[None, :] * (2 * steps[:, None] + odd)) % window)
        re, im = np.cos(angle) / math.sqrt(window), np.sin(angle) / math.sqrt(window)
        forms.append(np.block([[re, -im], [im, re]]))
    for turn in (0, 1):
        for form in forms:
            high, low = parts(form.T if turn else form)
            left.append(np.concatenate([high, high, low], 1))
            high, low = parts(form if turn else form.T)
            right.append(np.concatenate([high, high, low], 0))
    return np.stack(left), np.stack(right)


def halves(value):
    high = value.astype(BF16)
    low = (value - high.astype(F32)).astype(BF16)
    return high, low


def left_dot(table, value):
    high, low = halves(value)
    return jnp.dot(table, jnp.concatenate([high, low, high], 0), preferred_element_type=F32)


def right_dot(value, table):
    high, low = halves(value)
    return jnp.dot(jnp.concatenate([high, low, high], 1), table, preferred_element_type=F32)


def rows_cat(a, b):
    return jnp.concatenate([a, b], 0)


def lanes_cat(a, b):
    return jnp.concatenate([a, b], 1)


def forward(re, im, left, right):
    h = re.shape[0] // 2
    even = left_dot(left[0], rows_cat(re[:h] + re[h:], im[:h] + im[h:]))
    odd = left_dot(left[1], rows_cat(re[:h] - re[h:], im[:h] - im[h:]))
    re, im = rows_cat(even[:h], odd[:h]), rows_cat(even[h:], odd[h:])
    even = right_dot(lanes_cat(re[:, :h] + re[:, h:], im[:, :h] + im[:, h:]), right[0])
    odd = right_dot(lanes_cat(re[:, :h] - re[:, h:], im[:, :h] - im[:, h:]), right[1])
    return lanes_cat(even[:, :h], odd[:, :h]), lanes_cat(even[:, h:], odd[:, h:])


def backward(re, im, left, right):
    h = re.shape[0] // 2
    even = left_dot(left[2], rows_cat(re[:h], im[:h]))
    odd = left_dot(left[3], rows_cat(re[h:], im[h:]))
    plus, minus = even + odd, even - odd
    re, im = rows_cat(plus[:h], minus[:h]), rows_cat(plus[h:], minus[h:])
    even = right_dot(lanes_cat(re[:, :h], im[:, :h]), right[2])
    odd = right_dot(lanes_cat(re[:, h:], im[:, h:]), right[3])
    plus, minus = even + odd, even - odd
    return lanes_cat(plus[:, :h], minus[:, :h]), lanes_cat(plus[:, h:], minus[:, h:])


def place(offsets, q):
    row, col = offsets[q, 0], offsets[q, 1]
    start = pl.multiple_of((col // 128) * 128, 128)
    return row, start, col - start


def read_window(field, offsets, q, window):
    row, start, lane = place(offsets, q)
    rows, span = field.shape[1], window + 128
    found = []
    for p in range(2):
        block = field[p, :, pl.ds(start, span)].astype(F32)
        block = pltpu.roll(block, lax.rem(span - lane, span), 1)[:, :window]
        found.append(pltpu.roll(block, lax.rem(rows - row, rows), 0)[:window])
    return found


def add_window(field, offsets, q, terms):
    row, start, lane = place(offsets, q)
    window = terms[0].shape[0]
    rows, span = field.shape[1], window + 128
    for p in range(2):
        block = jnp.concatenate([terms[p], jnp.zeros((rows - window, window), F32)], 0)
        block = pltpu.roll(block, row, 0)
        block = jnp.concatenate([block, jnp.zeros((rows, span - window), F32)], 1)
        field[p, :, pl.ds(start, span)] += pltpu.roll(block, lane, 1)


def first_kernel(offsets, live, field, probe, prop, left, right, wave, trans):
    window = probe.shape[-1]

    def slot(q, _):
        t_re, t_im = read_window(field, offsets, q, window)
        trans[q, 0] = t_re.astype(BF16)
        trans[q, 1] = t_im.astype(BF16)
        p_re, p_im = probe[0], probe[1]
        re, im = forward(p_re * t_re - p_im * t_im, p_re * t_im + p_im * t_re, left, right)
        h_re, h_im = prop[0], prop[1]
        re, im = backward(re * h_re - im * h_im, re * h_im + im * h_re, left, right)
        wave[q, 0] = re
        wave[q, 1] = im
        return 0

    lax.fori_loop(0, live[0, 0], slot, 0)


def middle_kernel(offsets, live, field, wave, measured, left, right, gradient, carry):
    window = wave.shape[-1]
    gradient[...] = jnp.zeros(gradient.shape, F32)

    def slot(q, _):
        t_re, t_im = read_window(field, offsets, q, window)
        w_re, w_im = wave[q, 0], wave[q, 1]
        re, im = forward(w_re * t_re - w_im * t_im, w_re * t_im + w_im * t_re, left, right)
        residual = 2.0 * (re * re + im * im - measured[q].astype(F32))
        re, im = backward(residual * re, residual * im, left, right)
        w_re, w_im = wave[q, 0], wave[q, 1]
        add_window(gradient, offsets, q, (w_re * re + w_im * im, w_re * im - w_im * re))
        carry[q, 0] = t_re * re + t_im * im
        carry[q, 1] = t_re * im - t_im * re
        return 0

    lax.fori_loop(0, live[0, 0], slot, 0)


def last_kernel(offsets, live, carry, trans, probe, prop, left, right, gradient, total):
    gradient[...] = jnp.zeros(gradient.shape, F32)
    total[...] = jnp.zeros(total.shape, F32)

    def slot(q, _):
        re, im = forward(carry[q, 0], carry[q, 1], left, right)
        h_re, h_im = prop[0], prop[1]
        re, im = backward(re * h_re + im * h_im, im * h_re - re * h_im, left, right)
        p_re, p_im = probe[0], probe[1]
        add_window(gradient, offsets, q, (p_re * re + p_im * im, p_re * im - p_im * re))
        t_re, t_im = trans[q, 0].astype(F32), trans[q, 1].astype(F32)
        total[0] += t_re * re + t_im * im
        total[1] += t_re * im - t_im * re
        return 0

    lax.fori_loop(0, live[0, 0], slot, 0)


def call(kernel, outs, name, flops, *args):
    moved = sum(math.prod(a.shape) * a.dtype.itemsize for a in (*args, *outs))
    return pl.pallas_call(
        kernel,
        out_shape=outs,
        in_specs=[SCALARS] * 2 + [WHOLE] * (len(args) - 2),
        out_specs=[WHOLE] * len(outs),
        compiler_params=pltpu.CompilerParams(vmem_limit_bytes=48 * 1024 * 1024),
        cost_estimate=pl.CostEstimate(flops=flops, bytes_accessed=moved, transcendentals=0),
        name=name,
    )(*args)


def halo_rows(cells):
    above = passed_along(cells, "sy", 1)
    below = passed_along(cells, "sy", -1)
    return jnp.concatenate([above, cells, below], 1)


def halo_columns(cells, margin):
    from_left = passed_along(cells[:, :, cells.shape[2] - margin :], "sx", 1)
    from_right = passed_along(cells[:, :, :margin], "sx", -1)
    return jnp.concatenate([from_left, cells, from_right], 2)


def coded(block):
    top = jnp.max(jnp.abs(block), axis=1, keepdims=True)
    step = top * (1.0 / 32767.0)
    inverse = jnp.where(top > 1e-30, 32767.0 / jnp.where(top > 1e-30, top, 1.0), 0.0)
    return jnp.round(block * inverse).astype(jnp.int16), step


def sent_rows(block, distance):
    code, step = coded(block)
    code, step = passed_along(code, "sy", distance), passed_along(step, "sy", distance)
    return code.astype(F32) * step


def returned(gradient, margin):
    wide = gradient.shape[2]
    to_left, to_right = gradient[:, :, :margin], gradient[:, :, wide - margin :]
    from_right = passed_along(to_left, "sx", -1)
    from_left = passed_along(to_right, "sx", 1)
    inner = gradient[:, :, margin : wide - margin]
    inner = jnp.concatenate(
        [
            inner[:, :, :margin] + from_left,
            inner[:, :, margin:-margin],
            inner[:, :, -margin:] + from_right,
        ],
        2,
    )
    above, own, below = inner[:, :margin], inner[:, margin : 2 * margin], inner[:, 2 * margin :]
    return own + sent_rows(above, -1) + sent_rows(below, 1)


def shards(object_slices, probe_wave, propagator_phase, intensities, scan_offsets, live_counts):
    window = probe_wave.shape[-1]
    half = window // 2
    slots = scan_offsets.shape[2]
    offsets = scan_offsets[0, 0]

    first_field = halo_rows(object_slices[0])
    second_cells, first_field = lax.optimization_barrier((object_slices[1], first_field))
    second_field = halo_rows(second_cells)
    first_field = halo_columns(first_field, half)
    second_field = halo_columns(second_field, half)

    left, right = split_tables(window)
    left, right = jnp.asarray(left), jnp.asarray(right)
    order = np.concatenate([np.arange(0, window, 2), np.arange(1, window, 2)])
    pick = jnp.asarray(np.eye(window)[order], BF16)
    measured = jnp.einsum(
        "aj,qjk->qak", pick, intensities[0, 0], preferred_element_type=F32
    ).astype(BF16)
    measured = jnp.einsum("qak,bk->qab", measured, pick, preferred_element_type=F32).astype(BF16)
    phase = propagator_phase.reshape(half, 2, half, 2).transpose(1, 0, 3, 2).reshape(window, window)
    prop = jnp.stack([jnp.cos(phase), jnp.sin(phase)])

    flops = slots * 24 * 2 * window**3
    per_slot = jax.ShapeDtypeStruct((slots, 2, window, window), F32)
    per_slot_short = jax.ShapeDtypeStruct((slots, 2, window, window), BF16)
    whole_field = jax.ShapeDtypeStruct(first_field.shape, F32)
    pair = jax.ShapeDtypeStruct((2, window, window), F32)
    wave, trans = call(
        first_kernel, [per_slot, per_slot_short], "first", flops,
        offsets, live_counts, first_field, probe_wave, prop, left, right,
    )
    second_gradient, carry = call(
        middle_kernel, [whole_field, per_slot], "middle", flops,
        offsets, live_counts, second_field, wave, measured, left, right,
    )
    first_gradient, total = call(
        last_kernel, [whole_field, pair], "last", flops,
        offsets, live_counts, carry, trans, probe_wave, prop, left, right,
    )
    scale = 1.0 / math.sqrt(slots * lax.axis_size("sy") * lax.axis_size("sx"))
    probe_gradient = lax.psum(total, ("sy", "sx")) * scale
    gradient = jnp.stack([returned(first_gradient, half), returned(second_gradient, half)])
    return (gradient, probe_gradient)


def solution(mesh):
    return jax.shard_map(
        shards,
        mesh=mesh,
        in_specs=(
            P(None, None, "sy", "sx"),
            P(),
            P(),
            P("sy", "sx", None, None, None),
            P("sy", "sx", None, None),
            P("sy", "sx"),
        ),
        out_specs=(P(None, None, "sy", "sx"), P()),
        check_vma=False,
    )
```
